32 devices in a mesh: cells: 8 (over z, y), tracers: 4 (over x, core).
Axes of the slice: x: 2, y: 2, z: 4, core: 2. Of those that a mesh axis runs over, the one named last changes fastest.
Arguments:
- pulses: float32 [4096, 32, 128], P('tracers', 'cells'), may hold values from -6 to 6
- wind_x: float32 [32, 128], P('cells'), may hold values from -0.24 to 0.24
- wind_y: float32 [32, 128], P('cells'), may hold values from -0.24 to 0.24
- obs_tile: int32 [1024, 1], P('cells'), may hold values from 0 to 7; in each aligned block of 128 rows (0 to 127, 128 to 255, ...) at most 32 rows name the same one
- obs_weight: bfloat16 [1024, 512], P('cells'), may hold values from 0.099609375 to 10
- obs_precision: bfloat16 [1024], P('cells'), may hold values from 0.0029907227 to 0.099609375
Outputs:
- gram: float32 [4096, 4096], P('cells', 'tracers')
The draws below stay inside these ranges and needn't reach their ends.
Inputs may be any that keep to these rules, and one draw needn't show every extreme that they name: `obs_tile`: among the rows of one index of cells no tile is named by more than 32 rows, a bound that some block reaches of them.
All inputs are finite; a program needn't handle non-finite values.
Results may differ from the reference program's by a relative error of at most 0.0031.
Values may be sent and summed in bfloat16 or wider, within the bound.
A program may use at most 64 MiB of HBM per device.

```python
import math
import jax
import jax.numpy as jnp
import numpy as np
from jax import lax

K = 4096
ROWS_DEV = 4
COLS = 128
STEPS = 3
OBS_DEV = 128
ROWS = 32
TILE = 512
OBS = 1024
CAP = 32
N_CELLS = 8


def shard_levels(key, extent, cuts, smallest, largest):
    factor_of = 1.0
    for position, blocks in cuts:
        steps = jax.random.uniform(jax.random.fold_in(jax.random.fold_in(key, 6), position), (blocks,), jnp.float32, smallest / len(cuts), largest / len(cuts))
        factor_of = factor_of * jnp.repeat(jnp.exp(steps), extent[position] // blocks).reshape((-1,) + (1,) * (len(extent) - 1 - position))
    return factor_of


def shared_out(rng, own, number, rows, amount, top, bound, skew):
    order = jax.random.permutation(rng, amount)
    packed, usual = portions_of(amount, rows * top, bound, skew, True), portions_of(amount, rows * top, bound, skew, False)
    places = jnp.arange(amount)

    def named(tallies, offset_by):
        used = int((tallies > 0).sum())
        fixed = max(1, used // 4)
        moved = fixed + (places - fixed + offset_by * (used - fixed)) % max(1, amount - fixed)
        return jnp.zeros((amount,), jnp.int32).at[order[jnp.where(places < fixed, places, moved)]].set(jnp.asarray(tallies, jnp.int32))

    tallies = jnp.where(number % 4 == 0, named(packed, number // 4), named(usual, number - number // 4 - 1))
    mixed = jax.random.permutation(jax.random.fold_in(own, 3), amount)
    giver, receiver = mixed[0:amount // 2 * 2:2], mixed[1:amount // 2 * 2:2]
    margin = jnp.minimum(tallies[giver] - 1, bound - tallies[receiver]) // 2
    margin = jnp.where((giver == order[0]) | (receiver == order[0]) | (tallies[receiver] == 0), 0, jnp.maximum(margin, 0))
    moved = jax.random.randint(jax.random.fold_in(own, 4), (amount // 2,), 0, 1 << 20) % (margin + 1)
    tallies = tallies.at[giver].add(-moved).at[receiver].add(moved)
    labels = jnp.searchsorted(jnp.cumsum(tallies), jnp.arange(rows * top), side="right").astype(jnp.int32)
    listing = labels.reshape(top, rows).T
    listing = listing[jax.random.permutation(jax.random.fold_in(own, 1), rows)]
    offset_by = jax.random.randint(jax.random.fold_in(own, 2), (rows, 1), 0, top)
    return jnp.take_along_axis(listing, (jnp.arange(top)[None, :] + offset_by) % top, axis=1)


def portions_of(number_of, total, bound, skew, full):
    loads = [(1 << 20) // math.isqrt(standing ** skew) + 1 for standing in range(1, number_of + 1)]
    largest = bound if full else min(bound, max(-(-total // number_of), total * loads[0] // sum(loads)))
    least = 1 if total - largest >= number_of - 1 else 0
    holding, rest = [largest] + [least] * (number_of - 1), total - largest - least * (number_of - 1)
    while rest > 0:
        free = [i for i in range(1, number_of) if holding[i] < largest] or [i for i in range(1, number_of) if holding[i] < bound]
        whole, budget = sum([loads[i] for i in free]), rest
        for i in free:
            addition = min(bound - holding[i], max(1, budget * loads[i] // whole), rest)
            holding[i] = holding[i] + addition
            rest = rest - addition
    return np.array(holding)


def bell_draw(own_key, extent, scale, bound, cuts=(), kind=jnp.bfloat16):
    entries = jax.random.normal(own_key, extent, jnp.float32) * scale
    if len(cuts) > 0:
        entries = shard_levels(own_key, extent, cuts, -0.22, 0.18) * entries
    return jnp.clip(entries, min=-bound, max=bound).astype(kind)


def setup_inputs(seed: int = 0) -> dict:
    key_list = jax.random.split(jax.random.key(seed), 7)
    pulses = bell_draw(key_list[0], (K, ROWS, COLS), 1.0, 6.0, ((0, 4), (1, 8)), jnp.float32)
    wind_x = jnp.clip(jax.random.uniform(key_list[1], (ROWS, COLS), jnp.float32, -0.24, 0.24) * shard_levels(key_list[1], (ROWS, COLS), ((0, 8),), -0.4, 0.0), -0.24, 0.24)
    wind_y = jnp.clip(jax.random.uniform(key_list[2], (ROWS, COLS), jnp.float32, -0.24, 0.24) * shard_levels(key_list[2], (ROWS, COLS), ((0, 8),), -0.4, 0.0), -0.24, 0.24)
    obs_tile_keys = jax.random.split(jax.random.fold_in(key_list[3], 1), OBS // OBS_DEV)
    obs_tile_turns = jax.random.permutation(jax.random.fold_in(key_list[3], 3), OBS // OBS_DEV)
    obs_tile = jax.vmap(lambda own, number: shared_out(jax.random.fold_in(key_list[3], 2), own, number, OBS_DEV, N_CELLS, 1, CAP, 2))(obs_tile_keys, obs_tile_turns).reshape((OBS, 1))
    obs_weight = jnp.clip(jnp.exp(math.log(10.0) - 4.609084 * jax.random.uniform(key_list[4], (OBS, TILE), jnp.float32) ** shard_levels(key_list[4], (OBS, TILE), ((0, 8),), -0.2, 0.2)), 0.099609375, 10.0).astype(jnp.bfloat16)
    obs_precision = jnp.clip(jnp.exp(math.log(0.099609375) - 3.5057412 * jax.random.uniform(key_list[5], (OBS,), jnp.float32) ** shard_levels(key_list[5], (OBS,), ((0, 8),), -0.2, 0.2)), 0.0029907227, 0.099609375).astype(jnp.bfloat16)
    return {"pulses": pulses, "wind_x": wind_x, "wind_y": wind_y, "obs_tile": obs_tile, "obs_weight": obs_weight, "obs_precision": obs_precision}


def transport(tracer_field, wind_x, wind_y):
    for index_step in range(STEPS):
        behind = jnp.roll(tracer_field, 1, axis=2)
        flux_x = jnp.maximum(wind_x, 0.0) * behind + jnp.minimum(wind_x, 0.0) * tracer_field
        row_above = jnp.roll(tracer_field, 1, axis=1)
        flux_y = jnp.maximum(wind_y, 0.0) * row_above + jnp.minimum(wind_y, 0.0) * tracer_field
        tracer_field = tracer_field + flux_x - jnp.roll(flux_x, -1, axis=2) + flux_y - jnp.roll(flux_y, -1, axis=1)
    return tracer_field


def reference(pulses, wind_x, wind_y, obs_tile, obs_weight, obs_precision):
    blocks = pulses.reshape(K // 64, 64, ROWS, COLS)
    advected = lax.map(lambda block_one: transport(block_one, wind_x, wind_y).astype(jnp.bfloat16), blocks)
    final_field = advected.reshape(K, ROWS, COLS)
    weights_wide = obs_weight.astype(jnp.float32)
    averaging = (weights_wide / jnp.sum(weights_wide, axis=1, keepdims=True)).astype(jnp.bfloat16)
    tile_index = obs_tile[:, 0]
    slot_total = 2 * OBS_DEV
    precision_wide = obs_precision.astype(jnp.float32)

    def per_tile(carry_rows, tile_number):
        jac_all, weighted_all = carry_rows
        matches = tile_index == tile_number
        found_rows = jnp.nonzero(matches, size=slot_total, fill_value=0)[0].astype(jnp.int32)
        live_count = jnp.sum(matches.astype(jnp.int32))
        live_slot = jnp.arange(slot_total, dtype=jnp.int32) < live_count
        sampled = lax.dynamic_slice_in_dim(final_field, (tile_number * ROWS_DEV).astype(jnp.int32), ROWS_DEV, 1)
        sampled = sampled.reshape(K, ROWS_DEV * COLS)
        jac_tile = jnp.dot(averaging[found_rows], sampled.T, preferred_element_type=jnp.float32).astype(jnp.bfloat16)
        weighted_tile = (precision_wide[found_rows][:, None] * jac_tile.astype(jnp.float32)).astype(jnp.bfloat16)
        target = jnp.where(live_slot, found_rows, OBS).astype(jnp.int32)
        jac_all = jac_all.at[target].set(jac_tile, mode="drop")
        weighted_all = weighted_all.at[target].set(weighted_tile, mode="drop")
        return (jac_all, weighted_all), None

    start_rows = (jnp.zeros((OBS, K), jnp.bfloat16), jnp.zeros((OBS, K), jnp.bfloat16))
    (jac_all, weighted_all), unused = lax.scan(per_tile, start_rows, jnp.arange(N_CELLS, dtype=jnp.int32))
    return jnp.dot(jac_all.T, weighted_all, preferred_element_type=jnp.float32)
```

```python
import jax
import jax.numpy as jnp
from jax import lax
from jax.sharding import PartitionSpec as P

STEPS = 3


def advance(field, wx, wy):
    behind = jnp.roll(field, 1, axis=2)
    flux_x = jnp.maximum(wx, 0.0) * behind + jnp.minimum(wx, 0.0) * field
    above = jnp.roll(field, 1, axis=1)
    flux_y = jnp.maximum(wy, 0.0) * above + jnp.minimum(wy, 0.0) * field
    return field + flux_x - jnp.roll(flux_x, -1, axis=2) + flux_y - jnp.roll(flux_y, -1, axis=1)


def by_collectives(pulses, wind_x, wind_y, obs_tile, obs_weight, obs_precision):
    cells = lax.axis_size("cells")
    field = lax.all_to_all(pulses, "cells", split_axis=0, concat_axis=1, tiled=True)
    wx = lax.all_gather(wind_x, "cells", axis=0, tiled=True)
    wy = lax.all_gather(wind_y, "cells", axis=0, tiled=True)
    weights = obs_weight.astype(jnp.float32)
    averaging = (weights / jnp.sum(weights, axis=1, keepdims=True)).astype(jnp.bfloat16)
    averaging = lax.all_gather(averaging, "cells", axis=0, tiled=True)
    tile = lax.all_gather(obs_tile[:, 0], "cells", axis=0, tiled=True)
    precision = lax.all_gather(obs_precision, "cells", axis=0, tiled=True)
    for _ in range(STEPS):
        field = advance(field, wx, wy)
    tracers = field.shape[0]
    sampled = field.astype(jnp.bfloat16).reshape(tracers, cells, -1)

    def one_tile(t, total):
        part = lax.dot_general(
            lax.dynamic_index_in_dim(sampled, t, 1, keepdims=False),
            averaging,
            (((1,), (1,)), ((), ())),
            preferred_element_type=jnp.float32,
        )
        return jnp.where(tile[None, :] == t, part, total)

    total = lax.fori_loop(
        0, cells, one_tile, jnp.zeros((tracers, averaging.shape[0]), jnp.float32)
    )
    scaled = (total * jnp.sqrt(precision.astype(jnp.float32))[None, :]).astype(jnp.bfloat16)
    group = lax.all_gather(scaled, "cells", axis=0, tiled=True)
    count = group.shape[0] * lax.axis_size("tracers") // cells
    start = lax.axis_index("cells") * count
    owner, offset = start // group.shape[0], start % group.shape[0]
    mine = lax.dynamic_slice_in_dim(group, offset, count, 0)
    mine = jnp.where(lax.axis_index("tracers") == owner, mine, jnp.zeros_like(mine))
    mine = lax.psum(mine, "tracers")
    return lax.dot_general(
        mine, group, (((1,), (1,)), ((), ())), preferred_element_type=jnp.float32
    )


def solution(mesh):
    placed = (
        P("tracers", "cells", None),
        P("cells", None),
        P("cells", None),
        P("cells", None),
        P("cells", None),
        P("cells"),
    )
    return jax.shard_map(
        by_collectives, mesh=mesh, in_specs=placed, out_specs=P("cells", "tracers"), check_vma=False
    )
```

```python
import functools

import jax
import jax.numpy as jnp
from jax import lax
from jax.experimental import pallas as pl
from jax.experimental.pallas import tpu as pltpu
from jax.sharding import PartitionSpec as P

STEPS = 3
LEVELS = 32767.0
MESH = pl.DeviceIdType.MESH


def advance(field, wx, wy):
    behind = jnp.roll(field, 1, axis=2)
    flux_x = jnp.maximum(wx, 0.0) * behind + jnp.minimum(wx, 0.0) * field
    above = jnp.roll(field, 1, axis=1)
    flux_y = jnp.maximum(wy, 0.0) * above + jnp.minimum(wy, 0.0) * field
    return field + flux_x - jnp.roll(flux_x, -1, axis=2) + flux_y - jnp.roll(flux_y, -1, axis=1)


def by_collectives(pulses, wind_x, wind_y, obs_tile, obs_weight, obs_precision):
    cells = lax.axis_size("cells")
    field = lax.all_to_all(pulses, "cells", split_axis=0, concat_axis=1, tiled=True)
    wx = lax.all_gather(wind_x, "cells", axis=0, tiled=True)
    wy = lax.all_gather(wind_y, "cells", axis=0, tiled=True)
    weights = obs_weight.astype(jnp.float32)
    averaging = (weights / jnp.sum(weights, axis=1, keepdims=True)).astype(jnp.bfloat16)
    averaging = lax.all_gather(averaging, "cells", axis=0, tiled=True)
    tile = lax.all_gather(obs_tile[:, 0], "cells", axis=0, tiled=True)
    precision = lax.all_gather(obs_precision, "cells", axis=0, tiled=True)
    for _ in range(STEPS):
        field = advance(field, wx, wy)
    tracers = field.shape[0]
    sampled = field.astype(jnp.bfloat16).reshape(tracers, cells, -1)

    def one_tile(t, total):
        part = lax.dot_general(
            lax.dynamic_index_in_dim(sampled, t, 1, keepdims=False),
            averaging,
            (((1,), (1,)), ((), ())),
            preferred_element_type=jnp.float32,
        )
        return jnp.where(tile[None, :] == t, part, total)

    total = lax.fori_loop(
        0, cells, one_tile, jnp.zeros((tracers, averaging.shape[0]), jnp.float32)
    )
    scaled = (total * jnp.sqrt(precision.astype(jnp.float32))[None, :]).astype(jnp.bfloat16)
    group = lax.all_gather(scaled, "cells", axis=0, tiled=True)
    count = group.shape[0] * lax.axis_size("tracers") // cells
    start = lax.axis_index("cells") * count
    owner, offset = start // group.shape[0], start % group.shape[0]
    mine = lax.dynamic_slice_in_dim(group, offset, count, 0)
    mine = jnp.where(lax.axis_index("tracers") == owner, mine, jnp.zeros_like(mine))
    mine = lax.psum(mine, "tracers")
    return lax.dot_general(
        mine, group, (((1,), (1,)), ((), ())), preferred_element_type=jnp.float32
    )


def kernel(
    n, groups, rows,
    q_ref, small_ref, weight_ref, out_ref,
    q_send, q_recv, field_a, field_b, sampled, coef, averaging, meta, gathered, mine,
    q_ssem, q_rsem, m_ssem, m_rsem, a_ssem, a_rsem, f_ssem, f_rsem,
    up_s, up_r, down_s, down_r, y_s, y_r, k_s, k_r,
):
    c, g = lax.axis_index("cells"), lax.axis_index("tracers")
    depth = n // 2
    z, y = c // 2, c % 2
    k = q_ref.shape[0] // (rows * n)
    cols = q_ref.shape[1]
    quarter = averaging.shape[1] // groups
    obs = meta.shape[2]

    def to(cell, tracer):
        return (cell, tracer)

    barrier = pltpu.get_barrier_semaphore()
    for d in range(1, n):
        pl.semaphore_signal(barrier, inc=1, device_id=to((c + d) % n, g), device_id_type=MESH)
    for e in range(1, groups):
        pl.semaphore_signal(barrier, inc=1, device_id=to(c, (g + e) % groups), device_id_type=MESH)

    wide = weight_ref[...].astype(jnp.float32)
    wide = wide / jnp.sum(wide, axis=1, keepdims=True)
    averaging[c] = wide.T.astype(jnp.bfloat16)
    largest = jnp.max(jnp.abs(q_ref[...]), axis=0, keepdims=True)
    largest = jnp.maximum(jnp.max(largest, axis=1, keepdims=True), 1e-30)
    scale = largest * (1.0 / LEVELS)
    meta[c] = small_ref[...]
    meta[c, 10:11, :] = jnp.broadcast_to(scale, (1, obs))
    factor = jnp.broadcast_to(LEVELS / largest, (1, cols))

    pl.semaphore_wait(barrier, n - 1 + groups - 1)

    def remote(src, dst, ssem, rsem, device):
        return pltpu.make_async_remote_copy(
            src_ref=src, dst_ref=dst, send_sem=ssem, recv_sem=rsem,
            device_id=device, device_id_type=MESH,
        )

    def rows_of(group):
        return pl.ds(pl.multiple_of(group * quarter, quarter), quarter)

    def a_copy(d, source, target):
        ref = averaging.at[source, rows_of(g)]
        return remote(ref, ref, a_ssem.at[d], a_rsem.at[d], to(target, g))

    def m_copy(d, source, target):
        return remote(meta.at[source], meta.at[source], m_ssem.at[d], m_rsem.at[d], to(target, g))

    def q_copy(d, source, target):
        return remote(q_send.at[target], q_recv.at[source], q_ssem.at[d], q_rsem.at[d], to(target, g))

    def f_copy(d, e, source, group, target):
        ref = averaging.at[source, rows_of(group)]
        return remote(ref, ref, f_ssem.at[e, d], f_rsem.at[e, d], to(c, target))

    for d in range(1, n):
        a_copy(d, c, (c + d) % n).start()
        m_copy(d, c, (c + d) % n).start()
    for d in range(1, n):
        target = (c + d) % n
        for r in range(rows):
            part = q_ref[pl.ds(target * (k * rows) + r, k, stride=rows), :]
            q_send[target, r] = jnp.round(part * factor).astype(jnp.int32).astype(jnp.int16)
        q_copy(d, c, target).start()
    for r in range(rows):
        field_a[c * rows + r] = q_ref[pl.ds(c * (k * rows) + r, k, stride=rows), :]

    for d in range(1, n):
        source = (c + n - d) % n
        a_copy(d, source, (c + d) % n).wait_recv()
        for e in range(1, groups):
            f_copy(d, e, source, g, (g + e) % groups).start()
    for d in range(1, n):
        source = (c + n - d) % n
        m_copy(d, source, (c + d) % n).wait_recv()
    for d in range(1, n):
        source = (c + n - d) % n
        q_copy(d, source, (c + d) % n).wait_recv()
        unit = meta[source, 10:11, :]
        for r in range(rows):
            field_a[source * rows + r] = (
                q_recv[source, r].astype(jnp.int32).astype(jnp.float32) * unit
            )

    total_rows = n * rows
    wx = jnp.concatenate([meta[s, 0:rows, :] for s in range(n)], axis=0)
    wy = jnp.concatenate([meta[s, rows : 2 * rows, :] for s in range(n)], axis=0)
    wx_next = pltpu.roll(wx, cols - 1, 1)
    wy_next = pltpu.roll(wy, total_rows - 1, 0)
    coef[0] = (
        1.0 + jnp.minimum(wx, 0.0) - jnp.maximum(wx_next, 0.0)
        + jnp.minimum(wy, 0.0) - jnp.maximum(wy_next, 0.0)
    )
    coef[1] = jnp.maximum(wx, 0.0)
    coef[2] = -jnp.minimum(wx_next, 0.0)
    coef[3] = jnp.maximum(wy, 0.0)
    coef[4] = -jnp.minimum(wy_next, 0.0)

    def advance_row(source, i):
        own = source[i]
        above, below = source[(i + total_rows - 1) % total_rows], source[(i + 1) % total_rows]
        return (
            own * coef[0, pl.ds(i, 1), :]
            + pltpu.roll(own, 1, 1) * coef[1, pl.ds(i, 1), :]
            + pltpu.roll(own, cols - 1, 1) * coef[2, pl.ds(i, 1), :]
            + above * coef[3, pl.ds(i, 1), :]
            + below * coef[4, pl.ds(i, 1), :]
        )

    source, target = field_a, field_b
    for _ in range(STEPS - 1):
        def one(i, carry, source=source, target=target):
            target[i] = advance_row(source, i)
            return carry
        lax.fori_loop(0, total_rows, one, 0)
        source, target = target, source

    def last(t, carry):
        for r in range(rows):
            sampled[pl.ds(pl.multiple_of(t * k, k), k), r * cols : (r + 1) * cols] = advance_row(
                source, t * rows + r
            ).astype(jnp.bfloat16)
        return carry
    lax.fori_loop(0, n, last, 0)

    for d in range(1, n):
        origin = (c + n - d) % n
        for e in range(1, groups):
            f_copy(d, e, origin, (g + groups - e) % groups, (g + e) % groups).wait_recv()

    for b in range(n // 2):
        right = jnp.concatenate([averaging[2 * b], averaging[2 * b + 1]], axis=1)
        tile = jnp.concatenate([meta[2 * b, 8:9, :], meta[2 * b + 1, 8:9, :]], axis=1)
        precision = jnp.concatenate([meta[2 * b, 9:10, :], meta[2 * b + 1, 9:10, :]], axis=1)
        part = jnp.dot(sampled[...], right, preferred_element_type=jnp.float32)
        rows_jac = part[0:k]
        for t in range(1, n):
            rows_jac = jnp.where(tile == float(t), part[t * k : (t + 1) * k], rows_jac)
        gathered[c, :, 2 * b * obs : (2 * b + 2) * obs] = (
            rows_jac * jnp.sqrt(precision)
        ).astype(jnp.bfloat16)

    per_group = n // groups
    owner = c // per_group
    dx, dc = (g // 2 + owner // 2) % 2, (g % 2 + owner % 2) % 2
    is_owner = jnp.logical_and(dx == 0, dc == 0)
    is_relay = jnp.logical_and(dx == 1, dc == 0)
    core_mate = (g // 2) * 2 + (g + 1) % 2
    chip_mate = (g + 2) % groups

    def k_copy(m, block, lane, target):
        return remote(block, mine.at[m], k_s.at[lane, m], k_r.at[m], to(c, target))

    def hand_on(block):
        @pl.when(jnp.logical_and(is_owner, block // groups == c % per_group))
        def _():
            m = block % groups
            k_copy(m, gathered.at[block], 1, chip_mate).start()
            k_copy(m, gathered.at[block], 0, core_mate).start()
            mine[m] = gathered[block]

    def line(h, zz, target, s, r):
        ref = gathered.at[zz * 2 + y]
        return remote(ref, ref, s.at[h], r.at[h], to(target, g))

    above_z, below_z = (c + 2) % n, (c + n - 2) % n
    other = z * 2 + (1 - y)

    def y_copy(zz, yy):
        ref = gathered.at[zz * 2 + yy]
        return remote(ref, ref, y_s.at[zz], y_r.at[zz], to(other, g))

    def send_on(h, zz, is_up, is_down):
        if is_up:
            @pl.when(z < depth - 1)
            def _():
                line(h, zz, above_z, up_s, up_r).start()
        if is_down:
            @pl.when(z > 0)
            def _():
                line(h, zz, below_z, down_s, down_r).start()
        y_copy(zz, y).start()
        hand_on(zz * 2 + y)

    def take_y(zz):
        y_copy(zz, 1 - y).wait_recv()
        hand_on(zz * 2 + (1 - y))

    send_on(0, z, True, True)
    for h in range(depth):
        if h < depth - 1:
            @pl.when(z - 1 - h >= 0)
            def _():
                line(h, z - 1 - h, above_z, up_s, up_r).wait_recv()
                send_on(h + 1, z - 1 - h, True, False)

            @pl.when(z + 1 + h <= depth - 1)
            def _():
                line(h, z + 1 + h, below_z, down_s, down_r).wait_recv()
                send_on(h + 1, z + 1 + h, False, True)
        if h == 0:
            take_y(z)
        else:
            @pl.when(z - h >= 0)
            def _():
                take_y(z - h)

            @pl.when(z + h <= depth - 1)
            def _():
                take_y(z + h)

    @pl.when(jnp.logical_not(is_owner))
    def _():
        for m in range(groups):
            k_copy(m, mine.at[m], 0, core_mate).wait_recv()

            @pl.when(is_relay)
            def _():
                k_copy(m, mine.at[m], 0, core_mate).start()

    left = mine[...].reshape(groups * k, n * obs)
    for b in range(n // 2):
        right = gathered[2 * b : 2 * b + 2].reshape(2 * k, n * obs)
        out_ref[:, 2 * b * k : (2 * b + 2) * k] = lax.dot_general(
            left, right, (((1,), (1,)), ((), ())), preferred_element_type=jnp.float32
        )

    for d in range(1, n):
        a_copy(d, c, (c + d) % n).wait_send()
        m_copy(d, c, (c + d) % n).wait_send()
        q_copy(d, c, (c + d) % n).wait_send()
        for e in range(1, groups):
            f_copy(d, e, (c + n - d) % n, g, (g + e) % groups).wait_send()
    for h in range(depth):
        y_copy(h, y).wait_send()
        if h < depth - 1:
            @pl.when(jnp.logical_and(z < depth - 1, z - h >= 0))
            def _():
                line(h, z - h, above_z, up_s, up_r).wait_send()

            @pl.when(jnp.logical_and(z > 0, z + h <= depth - 1))
            def _():
                line(h, z + h, below_z, down_s, down_r).wait_send()
    for m in range(groups):
        @pl.when(is_owner)
        def _():
            k_copy(m, mine.at[m], 1, chip_mate).wait_send()

        @pl.when(jnp.logical_or(is_owner, is_relay))
        def _():
            k_copy(m, mine.at[m], 0, core_mate).wait_send()


def by_kernel(pulses, wind_x, wind_y, obs_tile, obs_weight, obs_precision):
    n, groups = lax.axis_size("cells"), lax.axis_size("tracers")
    tracers, rows, cols = pulses.shape
    obs, tile_cells = obs_weight.shape
    k = tracers // n
    small = jnp.concatenate(
        [
            wind_x,
            wind_y,
            obs_tile.reshape(1, obs).astype(jnp.float32),
            obs_precision.reshape(1, obs).astype(jnp.float32),
            jnp.zeros((2 * 8 - 2 * rows - 2, cols), jnp.float32),
        ],
        axis=0,
    )
    depth = n // 2
    dma = pltpu.SemaphoreType.DMA
    vmem = pl.BlockSpec(memory_space=pltpu.VMEM)
    return pl.pallas_call(
        functools.partial(kernel, n, groups, rows),
        out_shape=jax.ShapeDtypeStruct((groups * k, tracers), jnp.float32),
        in_specs=[vmem] * 3,
        out_specs=vmem,
        scratch_shapes=[
            pltpu.VMEM((n, rows, k, cols), jnp.int16),
            pltpu.VMEM((n, rows, k, cols), jnp.int16),
            pltpu.VMEM((n * rows, k, cols), jnp.float32),
            pltpu.VMEM((n * rows, k, cols), jnp.float32),
            pltpu.VMEM((n * k, rows * cols), jnp.bfloat16),
            pltpu.VMEM((5, n * rows, cols), jnp.float32),
            pltpu.VMEM((n, tile_cells, obs), jnp.bfloat16),
            pltpu.VMEM((n, small.shape[0], obs), jnp.float32),
            pltpu.VMEM((n, k, n * obs), jnp.bfloat16),
            pltpu.VMEM((groups, k, n * obs), jnp.bfloat16),
            dma((n,)), dma((n,)), dma((n,)), dma((n,)), dma((n,)), dma((n,)),
            dma((groups, n)), dma((groups, n)),
            dma((depth,)), dma((depth,)), dma((depth,)), dma((depth,)),
            dma((depth,)), dma((depth,)), dma((2, groups)), dma((groups,)),
        ],
        compiler_params=pltpu.CompilerParams(
            collective_id=0, has_side_effects=True, vmem_limit_bytes=48 << 20
        ),
        cost_estimate=pl.CostEstimate(
            flops=4 * n * obs * k * groups * tracers, bytes_accessed=8 << 20, transcendentals=0
        ),
    )(pulses.reshape(tracers * rows, cols), small, obs_weight)


def on_device(*args):
    n, groups = lax.axis_size("cells"), lax.axis_size("tracers")
    tracers, rows, cols = args[0].shape
    obs = args[4].shape[0]
    gathered = tracers * n * obs * 2
    fits = gathered <= 4 << 20 and tracers % (n * 16) == 0 and rows * 2 + 3 <= 16
    if fits and groups == 4 and n % groups == 0 and rows == 4 and obs == cols == 128:
        return by_kernel(*args)
    return by_collectives(*args)


def solution(mesh):
    placed = (
        P("tracers", "cells", None),
        P("cells", None),
        P("cells", None),
        P("cells", None),
        P("cells", None),
        P("cells"),
    )
    return jax.shard_map(
        on_device, mesh=mesh, in_specs=placed, out_specs=P("cells", "tracers"), check_vma=False
    )
```

```python
import functools

import jax
import jax.numpy as jnp
from jax import lax
from jax.experimental import pallas as pl
from jax.experimental.pallas import tpu as pltpu
from jax.sharding import PartitionSpec as P

STEPS = 3
CHUNKS = 2
LEVELS = 32767.0
MESH = pl.DeviceIdType.MESH


def advance(field, wx, wy):
    behind = jnp.roll(field, 1, axis=2)
    flux_x = jnp.maximum(wx, 0.0) * behind + jnp.minimum(wx, 0.0) * field
    above = jnp.roll(field, 1, axis=1)
    flux_y = jnp.maximum(wy, 0.0) * above + jnp.minimum(wy, 0.0) * field
    return field + flux_x - jnp.roll(flux_x, -1, axis=2) + flux_y - jnp.roll(flux_y, -1, axis=1)


def by_collectives(pulses, wind_x, wind_y, obs_tile, obs_weight, obs_precision):
    cells = lax.axis_size("cells")
    field = lax.all_to_all(pulses, "cells", split_axis=0, concat_axis=1, tiled=True)
    wx = lax.all_gather(wind_x, "cells", axis=0, tiled=True)
    wy = lax.all_gather(wind_y, "cells", axis=0, tiled=True)
    weights = obs_weight.astype(jnp.float32)
    averaging = (weights / jnp.sum(weights, axis=1, keepdims=True)).astype(jnp.bfloat16)
    averaging = lax.all_gather(averaging, "cells", axis=0, tiled=True)
    tile = lax.all_gather(obs_tile[:, 0], "cells", axis=0, tiled=True)
    precision = lax.all_gather(obs_precision, "cells", axis=0, tiled=True)
    for _ in range(STEPS):
        field = advance(field, wx, wy)
    tracers = field.shape[0]
    sampled = field.astype(jnp.bfloat16).reshape(tracers, cells, -1)

    def one_tile(t, total):
        part = lax.dot_general(
            lax.dynamic_index_in_dim(sampled, t, 1, keepdims=False),
            averaging,
            (((1,), (1,)), ((), ())),
            preferred_element_type=jnp.float32,
        )
        return jnp.where(tile[None, :] == t, part, total)

    total = lax.fori_loop(
        0, cells, one_tile, jnp.zeros((tracers, averaging.shape[0]), jnp.float32)
    )
    scaled = (total * jnp.sqrt(precision.astype(jnp.float32))[None, :]).astype(jnp.bfloat16)
    group = lax.all_gather(scaled, "cells", axis=0, tiled=True)
    count = group.shape[0] * lax.axis_size("tracers") // cells
    start = lax.axis_index("cells") * count
    owner, offset = start // group.shape[0], start % group.shape[0]
    mine = lax.dynamic_slice_in_dim(group, offset, count, 0)
    mine = jnp.where(lax.axis_index("tracers") == owner, mine, jnp.zeros_like(mine))
    mine = lax.psum(mine, "tracers")
    return lax.dot_general(
        mine, group, (((1,), (1,)), ((), ())), preferred_element_type=jnp.float32
    )


def kernel(
    n, groups, rows,
    q_ref, small_ref, weight_ref, out_ref,
    q_send, q_recv, field_a, field_b, sampled, coef, averaging, meta, gathered, mine,
    q_ssem, q_rsem, m_ssem, m_rsem, a_ssem, a_rsem, f_ssem, f_rsem,
    up_s, up_r, down_s, down_r, y_s, y_r, k_s, k_r,
):
    c, g = lax.axis_index("cells"), lax.axis_index("tracers")
    depth = n // 2
    z, y = c // 2, c % 2
    k = q_ref.shape[0] // (rows * n)
    part_k = k // CHUNKS
    cols = q_ref.shape[1]
    quarter = averaging.shape[1] // groups
    obs = meta.shape[2]

    def to(cell, tracer):
        return (cell, tracer)

    barrier = pltpu.get_barrier_semaphore()
    for d in range(1, n):
        pl.semaphore_signal(barrier, inc=1, device_id=to((c + d) % n, g), device_id_type=MESH)
    for e in range(1, groups):
        pl.semaphore_signal(barrier, inc=1, device_id=to(c, (g + e) % groups), device_id_type=MESH)

    wide = weight_ref[...].astype(jnp.float32)
    wide = wide / jnp.sum(wide, axis=1, keepdims=True)
    averaging[c] = wide.T.astype(jnp.bfloat16)
    largest = jnp.max(jnp.abs(q_ref[...]), axis=0, keepdims=True)
    largest = jnp.maximum(jnp.max(largest, axis=1, keepdims=True), 1e-30)
    scale = largest * (1.0 / LEVELS)
    meta[c] = small_ref[...]
    meta[c, 10:11, :] = jnp.broadcast_to(scale, (1, obs))
    factor = jnp.broadcast_to(LEVELS / largest, (1, cols))

    pl.semaphore_wait(barrier, n - 1 + groups - 1)

    def remote(src, dst, ssem, rsem, device):
        return pltpu.make_async_remote_copy(
            src_ref=src, dst_ref=dst, send_sem=ssem, recv_sem=rsem,
            device_id=device, device_id_type=MESH,
        )

    def rows_of(group):
        return pl.ds(pl.multiple_of(group * quarter, quarter), quarter)

    def a_copy(d, source, target):
        ref = averaging.at[source, rows_of(g)]
        return remote(ref, ref, a_ssem.at[d], a_rsem.at[d], to(target, g))

    def m_copy(d, source, target):
        return remote(meta.at[source], meta.at[source], m_ssem.at[d], m_rsem.at[d], to(target, g))

    def q_copy(p, d, source, target):
        return remote(
            q_send.at[p, target], q_recv.at[p, source], q_ssem.at[p, d], q_rsem.at[p, d], to(target, g)
        )

    def own_rows(p, target, r):
        return q_ref[pl.ds(target * (k * rows) + p * (part_k * rows) + r, part_k, stride=rows), :]

    def f_copy(d, e, source, group, target):
        ref = averaging.at[source, rows_of(group)]
        return remote(ref, ref, f_ssem.at[e, d], f_rsem.at[e, d], to(c, target))

    for d in range(1, n):
        a_copy(d, c, (c + d) % n).start()
        m_copy(d, c, (c + d) % n).start()
    for p in range(CHUNKS):
        for d in range(1, n):
            target = (c + d) % n
            for r in range(rows):
                whole = jnp.round(own_rows(p, target, r) * factor)
                q_send[p, target, r] = whole.astype(jnp.int32).astype(jnp.int16)
            q_copy(p, d, c, target).start()

    for d in range(1, n):
        source = (c + n - d) % n
        a_copy(d, source, (c + d) % n).wait_recv()
        for e in range(1, groups):
            f_copy(d, e, source, g, (g + e) % groups).start()
    for d in range(1, n):
        source = (c + n - d) % n
        m_copy(d, source, (c + d) % n).wait_recv()
    total_rows = n * rows
    wx = jnp.concatenate([meta[s, 0:rows, :] for s in range(n)], axis=0)
    wy = jnp.concatenate([meta[s, rows : 2 * rows, :] for s in range(n)], axis=0)
    wx_next = pltpu.roll(wx, cols - 1, 1)
    wy_next = pltpu.roll(wy, total_rows - 1, 0)
    coef[0] = (
        1.0 + jnp.minimum(wx, 0.0) - jnp.maximum(wx_next, 0.0)
        + jnp.minimum(wy, 0.0) - jnp.maximum(wy_next, 0.0)
    )
    coef[1] = jnp.maximum(wx, 0.0)
    coef[2] = -jnp.minimum(wx_next, 0.0)
    coef[3] = jnp.maximum(wy, 0.0)
    coef[4] = -jnp.minimum(wy_next, 0.0)

    def advance_row(source, i):
        own = source[i]
        above, below = source[(i + total_rows - 1) % total_rows], source[(i + 1) % total_rows]
        return (
            own * coef[0, pl.ds(i, 1), :]
            + pltpu.roll(own, 1, 1) * coef[1, pl.ds(i, 1), :]
            + pltpu.roll(own, cols - 1, 1) * coef[2, pl.ds(i, 1), :]
            + above * coef[3, pl.ds(i, 1), :]
            + below * coef[4, pl.ds(i, 1), :]
        )

    def take_pulses(p):
        for r in range(rows):
            field_a[c * rows + r] = own_rows(p, c, r)
        for d in range(1, n):
            origin = (c + n - d) % n
            q_copy(p, d, origin, (c + d) % n).wait_recv()
            unit = meta[origin, 10:11, :]
            for r in range(rows):
                field_a[origin * rows + r] = (
                    q_recv[p, origin, r].astype(jnp.int32).astype(jnp.float32) * unit
                )

    def transport():
        source, target = field_a, field_b
        for _ in range(STEPS - 1):
            def one(i, carry, source=source, target=target):
                target[i] = advance_row(source, i)
                return carry
            lax.fori_loop(0, total_rows, one, 0, unroll=4)
            source, target = target, source

        def last(t, carry):
            for r in range(rows):
                here = pl.ds(pl.multiple_of(t * part_k, part_k), part_k)
                sampled[here, r * cols : (r + 1) * cols] = advance_row(source, t * rows + r).astype(
                    jnp.bfloat16
                )
            return carry
        lax.fori_loop(0, n, last, 0)

    def take_averaging():
        for d in range(1, n):
            origin = (c + n - d) % n
            for e in range(1, groups):
                f_copy(d, e, origin, (g + groups - e) % groups, (g + e) % groups).wait_recv()

    def jacobian(p):
        for b in range(n // 2):
            right = jnp.concatenate([averaging[2 * b], averaging[2 * b + 1]], axis=1)
            tile = jnp.concatenate([meta[2 * b, 8:9, :], meta[2 * b + 1, 8:9, :]], axis=1)
            precision = jnp.concatenate([meta[2 * b, 9:10, :], meta[2 * b + 1, 9:10, :]], axis=1)
            product = jnp.dot(sampled[...], right, preferred_element_type=jnp.float32)
            rows_jac = product[0:part_k]
            for t in range(1, n):
                rows_jac = jnp.where(
                    tile == float(t), product[t * part_k : (t + 1) * part_k], rows_jac
                )
            gathered[c, p * part_k : (p + 1) * part_k, 2 * b * obs : (2 * b + 2) * obs] = (
                rows_jac * jnp.sqrt(precision)
            ).astype(jnp.bfloat16)

    per_group = n // groups
    owner = c // per_group
    dx, dc = (g // 2 + owner // 2) % 2, (g % 2 + owner % 2) % 2
    is_owner = jnp.logical_and(dx == 0, dc == 0)
    is_relay = jnp.logical_and(dx == 1, dc == 0)
    core_mate = (g // 2) * 2 + (g + 1) % 2
    chip_mate = (g + 2) % groups

    def piece(p):
        return pl.ds(p * part_k, part_k)

    def k_copy(p, m, source, lane, target):
        return remote(
            source, mine.at[m, piece(p)], k_s.at[p, lane, m], k_r.at[p, m], to(c, target)
        )

    def hand_on(p, block):
        @pl.when(jnp.logical_and(is_owner, block // groups == c % per_group))
        def _():
            m = block % groups
            k_copy(p, m, gathered.at[block, piece(p)], 1, chip_mate).start()
            k_copy(p, m, gathered.at[block, piece(p)], 0, core_mate).start()
            mine[m, piece(p)] = gathered[block, piece(p)]

    def line(p, h, zz, target, s, r):
        ref = gathered.at[zz * 2 + y, piece(p)]
        return remote(ref, ref, s.at[p, h], r.at[p, h], to(target, g))

    above_z, below_z = (c + 2) % n, (c + n - 2) % n
    other = z * 2 + (1 - y)

    def y_copy(p, zz, yy):
        ref = gathered.at[zz * 2 + yy, piece(p)]
        return remote(ref, ref, y_s.at[p, zz], y_r.at[p, zz], to(other, g))

    def send_on(p, h, zz, is_up, is_down):
        if is_up:
            @pl.when(z < depth - 1)
            def _():
                line(p, h, zz, above_z, up_s, up_r).start()
        if is_down:
            @pl.when(z > 0)
            def _():
                line(p, h, zz, below_z, down_s, down_r).start()
        y_copy(p, zz, y).start()
        hand_on(p, zz * 2 + y)

    def take_y(p, zz):
        y_copy(p, zz, 1 - y).wait_recv()
        hand_on(p, zz * 2 + (1 - y))

    def stage(p, h):
        if h < depth - 1:
            @pl.when(z - 1 - h >= 0)
            def _():
                line(p, h, z - 1 - h, above_z, up_s, up_r).wait_recv()
                send_on(p, h + 1, z - 1 - h, True, False)

            @pl.when(z + 1 + h <= depth - 1)
            def _():
                line(p, h, z + 1 + h, below_z, down_s, down_r).wait_recv()
                send_on(p, h + 1, z + 1 + h, False, True)
        if h == 0:
            take_y(p, z)
        else:
            @pl.when(z - h >= 0)
            def _():
                take_y(p, z - h)

            @pl.when(z + h <= depth - 1)
            def _():
                take_y(p, z + h)

    early = 1
    for p in range(CHUNKS):
        take_pulses(p)
        transport()
        if p == 0:
            take_averaging()
        jacobian(p)
        send_on(p, 0, z, True, True)
        if p > 0:
            for h in range(early, depth):
                stage(p - 1, h)
        for h in range(early if p < CHUNKS - 1 else depth):
            stage(p, h)

    @pl.when(jnp.logical_not(is_owner))
    def _():
        for p in range(CHUNKS):
            for m in range(groups):
                k_copy(p, m, mine.at[m, piece(p)], 0, core_mate).wait_recv()

                @pl.when(is_relay)
                def _():
                    k_copy(p, m, mine.at[m, piece(p)], 0, core_mate).start()

    left = mine[...].reshape(groups * k, n * obs)
    for b in range(n // 2):
        right = gathered[2 * b : 2 * b + 2].reshape(2 * k, n * obs)
        out_ref[:, 2 * b * k : (2 * b + 2) * k] = lax.dot_general(
            left, right, (((1,), (1,)), ((), ())), preferred_element_type=jnp.float32
        )

    for d in range(1, n):
        a_copy(d, c, (c + d) % n).wait_send()
        m_copy(d, c, (c + d) % n).wait_send()
        for p in range(CHUNKS):
            q_copy(p, d, c, (c + d) % n).wait_send()
        for e in range(1, groups):
            f_copy(d, e, (c + n - d) % n, g, (g + e) % groups).wait_send()
    for p in range(CHUNKS):
        for h in range(depth):
            y_copy(p, h, y).wait_send()
            if h < depth - 1:
                @pl.when(jnp.logical_and(z < depth - 1, z - h >= 0))
                def _():
                    line(p, h, z - h, above_z, up_s, up_r).wait_send()

                @pl.when(jnp.logical_and(z > 0, z + h <= depth - 1))
                def _():
                    line(p, h, z + h, below_z, down_s, down_r).wait_send()
        for m in range(groups):
            @pl.when(is_owner)
            def _():
                k_copy(p, m, mine.at[m, piece(p)], 1, chip_mate).wait_send()

            @pl.when(jnp.logical_or(is_owner, is_relay))
            def _():
                k_copy(p, m, mine.at[m, piece(p)], 0, core_mate).wait_send()


def by_kernel(pulses, wind_x, wind_y, obs_tile, obs_weight, obs_precision):
    n, groups = lax.axis_size("cells"), lax.axis_size("tracers")
    tracers, rows, cols = pulses.shape
    obs, tile_cells = obs_weight.shape
    k = tracers // n
    part_k = k // CHUNKS
    small = jnp.concatenate(
        [
            wind_x,
            wind_y,
            obs_tile.reshape(1, obs).astype(jnp.float32),
            obs_precision.reshape(1, obs).astype(jnp.float32),
            jnp.zeros((2 * 8 - 2 * rows - 2, cols), jnp.float32),
        ],
        axis=0,
    )
    depth = n // 2
    dma = pltpu.SemaphoreType.DMA
    vmem = pl.BlockSpec(memory_space=pltpu.VMEM)
    return pl.pallas_call(
        functools.partial(kernel, n, groups, rows),
        out_shape=jax.ShapeDtypeStruct((groups * k, tracers), jnp.float32),
        in_specs=[vmem] * 3,
        out_specs=vmem,
        scratch_shapes=[
            pltpu.VMEM((CHUNKS, n, rows, part_k, cols), jnp.int16),
            pltpu.VMEM((CHUNKS, n, rows, part_k, cols), jnp.int16),
            pltpu.VMEM((n * rows, part_k, cols), jnp.float32),
            pltpu.VMEM((n * rows, part_k, cols), jnp.float32),
            pltpu.VMEM((n * part_k, rows * cols), jnp.bfloat16),
            pltpu.VMEM((5, n * rows, cols), jnp.float32),
            pltpu.VMEM((n, tile_cells, obs), jnp.bfloat16),
            pltpu.VMEM((n, small.shape[0], obs), jnp.float32),
            pltpu.VMEM((n, k, n * obs), jnp.bfloat16),
            pltpu.VMEM((groups, k, n * obs), jnp.bfloat16),
            dma((CHUNKS, n)), dma((CHUNKS, n)), dma((n,)), dma((n,)), dma((n,)), dma((n,)),
            dma((groups, n)), dma((groups, n)),
            *[dma((CHUNKS, depth))] * 6,
            dma((CHUNKS, 2, groups)), dma((CHUNKS, groups)),
        ],
        compiler_params=pltpu.CompilerParams(
            collective_id=0, has_side_effects=True, vmem_limit_bytes=48 << 20
        ),
        cost_estimate=pl.CostEstimate(
            flops=4 * n * obs * k * groups * tracers, bytes_accessed=8 << 20, transcendentals=0
        ),
    )(pulses.reshape(tracers * rows, cols), small, obs_weight)


def on_device(*args):
    n, groups = lax.axis_size("cells"), lax.axis_size("tracers")
    tracers, rows, cols = args[0].shape
    obs = args[4].shape[0]
    gathered = tracers * n * obs * 2
    fits = gathered <= 4 << 20 and tracers % (n * 16 * CHUNKS) == 0 and rows * 2 + 3 <= 16
    if fits and groups == 4 and n % groups == 0 and rows == 4 and obs == cols == 128:
        return by_kernel(*args)
    return by_collectives(*args)


def solution(mesh):
    placed = (
        P("tracers", "cells", None),
        P("cells", None),
        P("cells", None),
        P("cells", None),
        P("cells", None),
        P("cells"),
    )
    return jax.shard_map(
        on_device, mesh=mesh, in_specs=placed, out_specs=P("cells", "tracers"), check_vma=False
    )
```

```python
import functools

import jax
import jax.numpy as jnp
from jax import lax
from jax.experimental import pallas as pl
from jax.experimental.pallas import tpu as pltpu
from jax.sharding import PartitionSpec as P

STEPS = 3
CHUNKS = 2
LEVELS = 32767.0
MESH = pl.DeviceIdType.MESH


def advance(field, wx, wy):
    behind = jnp.roll(field, 1, axis=2)
    flux_x = jnp.maximum(wx, 0.0) * behind + jnp.minimum(wx, 0.0) * field
    above = jnp.roll(field, 1, axis=1)
    flux_y = jnp.maximum(wy, 0.0) * above + jnp.minimum(wy, 0.0) * field
    return field + flux_x - jnp.roll(flux_x, -1, axis=2) + flux_y - jnp.roll(flux_y, -1, axis=1)


def by_collectives(pulses, wind_x, wind_y, obs_tile, obs_weight, obs_precision):
    cells = lax.axis_size("cells")
    field = lax.all_to_all(pulses, "cells", split_axis=0, concat_axis=1, tiled=True)
    wx = lax.all_gather(wind_x, "cells", axis=0, tiled=True)
    wy = lax.all_gather(wind_y, "cells", axis=0, tiled=True)
    weights = obs_weight.astype(jnp.float32)
    averaging = (weights / jnp.sum(weights, axis=1, keepdims=True)).astype(jnp.bfloat16)
    averaging = lax.all_gather(averaging, "cells", axis=0, tiled=True)
    tile = lax.all_gather(obs_tile[:, 0], "cells", axis=0, tiled=True)
    precision = lax.all_gather(obs_precision, "cells", axis=0, tiled=True)
    for _ in range(STEPS):
        field = advance(field, wx, wy)
    tracers = field.shape[0]
    sampled = field.astype(jnp.bfloat16).reshape(tracers, cells, -1)

    def one_tile(t, total):
        part = lax.dot_general(
            lax.dynamic_index_in_dim(sampled, t, 1, keepdims=False),
            averaging,
            (((1,), (1,)), ((), ())),
            preferred_element_type=jnp.float32,
        )
        return jnp.where(tile[None, :] == t, part, total)

    total = lax.fori_loop(
        0, cells, one_tile, jnp.zeros((tracers, averaging.shape[0]), jnp.float32)
    )
    scaled = (total * jnp.sqrt(precision.astype(jnp.float32))[None, :]).astype(jnp.bfloat16)
    group = lax.all_gather(scaled, "cells", axis=0, tiled=True)
    count = group.shape[0] * lax.axis_size("tracers") // cells
    start = lax.axis_index("cells") * count
    owner, offset = start // group.shape[0], start % group.shape[0]
    mine = lax.dynamic_slice_in_dim(group, offset, count, 0)
    mine = jnp.where(lax.axis_index("tracers") == owner, mine, jnp.zeros_like(mine))
    mine = lax.psum(mine, "tracers")
    return lax.dot_general(
        mine, group, (((1,), (1,)), ((), ())), preferred_element_type=jnp.float32
    )


def kernel(
    n, groups, rows,
    q_ref, small_ref, weight_ref, out_ref,
    q_send, q_recv, field_a, field_b, sampled, coef, averaging, meta, gathered, mine,
    q_ssem, q_rsem, m_ssem, m_rsem, a_ssem, a_rsem, f_ssem, f_rsem,
    up_s, up_r, down_s, down_r, y_s, y_r, k_s, k_r,
):
    c, g = lax.axis_index("cells"), lax.axis_index("tracers")
    depth = n // 2
    z, y = c // 2, c % 2
    k = q_ref.shape[0] // (rows * n)
    part_k = k // CHUNKS
    cols = q_ref.shape[1]
    quarter = averaging.shape[1] // groups
    obs = meta.shape[2]

    def to(cell, tracer):
        return (cell, tracer)

    barrier = pltpu.get_barrier_semaphore()
    for d in range(1, n):
        pl.semaphore_signal(barrier, inc=1, device_id=to((c + d) % n, g), device_id_type=MESH)
    for e in range(1, groups):
        pl.semaphore_signal(barrier, inc=1, device_id=to(c, (g + e) % groups), device_id_type=MESH)

    wide = weight_ref[...].astype(jnp.float32)
    wide = wide / jnp.sum(wide, axis=1, keepdims=True)
    averaging[c] = wide.T.astype(jnp.bfloat16)
    largest = jnp.max(jnp.abs(q_ref[...]), axis=0, keepdims=True)
    largest = jnp.maximum(jnp.max(largest, axis=1, keepdims=True), 1e-30)
    scale = largest * (1.0 / LEVELS)
    meta[c] = small_ref[...]
    meta[c, 10:11, :] = jnp.broadcast_to(scale, (1, obs))
    factor = jnp.broadcast_to(LEVELS / largest, (1, cols))

    pl.semaphore_wait(barrier, n - 1 + groups - 1)

    def remote(src, dst, ssem, rsem, device):
        return pltpu.make_async_remote_copy(
            src_ref=src, dst_ref=dst, send_sem=ssem, recv_sem=rsem,
            device_id=device, device_id_type=MESH,
        )

    def rows_of(group):
        return pl.ds(pl.multiple_of(group * quarter, quarter), quarter)

    def a_copy(d, source, target):
        ref = averaging.at[source, rows_of(g)]
        return remote(ref, ref, a_ssem.at[d], a_rsem.at[d], to(target, g))

    def m_copy(d, source, target):
        return remote(meta.at[source], meta.at[source], m_ssem.at[d], m_rsem.at[d], to(target, g))

    def q_copy(p, d, source, target):
        return remote(
            q_send.at[p, target], q_recv.at[p, source], q_ssem.at[p, d], q_rsem.at[p, d], to(target, g)
        )

    def own_rows(p, target, r):
        return q_ref[pl.ds(target * (k * rows) + p * (part_k * rows) + r, part_k, stride=rows), :]

    def f_copy(d, e, source, group, target):
        ref = averaging.at[source, rows_of(group)]
        return remote(ref, ref, f_ssem.at[e, d], f_rsem.at[e, d], to(c, target))

    for d in range(1, n):
        a_copy(d, c, (c + d) % n).start()
        m_copy(d, c, (c + d) % n).start()
    for p in range(CHUNKS):
        for d in range(1, n):
            target = (c + d) % n
            for r in range(rows):
                whole = jnp.round(own_rows(p, target, r) * factor)
                q_send[p, target, r] = whole.astype(jnp.int32).astype(jnp.int16)
            q_copy(p, d, c, target).start()

    for d in range(1, n):
        source = (c + n - d) % n
        a_copy(d, source, (c + d) % n).wait_recv()
        for e in range(1, groups):
            f_copy(d, e, source, g, (g + e) % groups).start()
    for d in range(1, n):
        source = (c + n - d) % n
        m_copy(d, source, (c + d) % n).wait_recv()
    total_rows = n * rows
    wx = jnp.concatenate([meta[s, 0:rows, :] for s in range(n)], axis=0)
    wy = jnp.concatenate([meta[s, rows : 2 * rows, :] for s in range(n)], axis=0)
    wx_next = pltpu.roll(wx, cols - 1, 1)
    wy_next = pltpu.roll(wy, total_rows - 1, 0)
    coef[0] = (
        1.0 + jnp.minimum(wx, 0.0) - jnp.maximum(wx_next, 0.0)
        + jnp.minimum(wy, 0.0) - jnp.maximum(wy_next, 0.0)
    )
    coef[1] = jnp.maximum(wx, 0.0)
    coef[2] = -jnp.minimum(wx_next, 0.0)
    coef[3] = jnp.maximum(wy, 0.0)
    coef[4] = -jnp.minimum(wy_next, 0.0)

    def advance_row(source, i):
        own = source[i]
        above, below = source[(i + total_rows - 1) % total_rows], source[(i + 1) % total_rows]
        return (
            own * coef[0, pl.ds(i, 1), :]
            + pltpu.roll(own, 1, 1) * coef[1, pl.ds(i, 1), :]
            + pltpu.roll(own, cols - 1, 1) * coef[2, pl.ds(i, 1), :]
            + above * coef[3, pl.ds(i, 1), :]
            + below * coef[4, pl.ds(i, 1), :]
        )

    def take_pulses(p):
        for r in range(rows):
            field_a[c * rows + r] = own_rows(p, c, r)
        for d in range(1, n):
            origin = (c + n - d) % n
            q_copy(p, d, origin, (c + d) % n).wait_recv()
            unit = meta[origin, 10:11, :]
            for r in range(rows):
                field_a[origin * rows + r] = (
                    q_recv[p, origin, r].astype(jnp.int32).astype(jnp.float32) * unit
                )

    def transport():
        source, target = field_a, field_b
        for _ in range(STEPS - 1):
            def one(i, carry, source=source, target=target):
                target[i] = advance_row(source, i)
                return carry
            lax.fori_loop(0, total_rows, one, 0, unroll=8)
            source, target = target, source

        def last(t, carry):
            for r in range(rows):
                here = pl.ds(pl.multiple_of(t * part_k, part_k), part_k)
                sampled[here, r * cols : (r + 1) * cols] = advance_row(source, t * rows + r).astype(
                    jnp.bfloat16
                )
            return carry
        lax.fori_loop(0, n, last, 0, unroll=2)

    def take_averaging():
        for d in range(1, n):
            origin = (c + n - d) % n
            for e in range(1, groups):
                f_copy(d, e, origin, (g + groups - e) % groups, (g + e) % groups).wait_recv()

    def jacobian(p):
        for b in range(n // 2):
            right = jnp.concatenate([averaging[2 * b], averaging[2 * b + 1]], axis=1)
            tile = jnp.concatenate([meta[2 * b, 8:9, :], meta[2 * b + 1, 8:9, :]], axis=1)
            precision = jnp.concatenate([meta[2 * b, 9:10, :], meta[2 * b + 1, 9:10, :]], axis=1)
            product = jnp.dot(sampled[...], right, preferred_element_type=jnp.float32)
            rows_jac = product[0:part_k]
            for t in range(1, n):
                rows_jac = jnp.where(
                    tile == float(t), product[t * part_k : (t + 1) * part_k], rows_jac
                )
            gathered[c, p * part_k : (p + 1) * part_k, 2 * b * obs : (2 * b + 2) * obs] = (
                rows_jac * jnp.sqrt(precision)
            ).astype(jnp.bfloat16)

    per_group = n // groups
    owner = c // per_group
    dx, dc = (g // 2 + owner // 2) % 2, (g % 2 + owner % 2) % 2
    is_owner = jnp.logical_and(dx == 0, dc == 0)
    is_relay = jnp.logical_and(dx == 1, dc == 0)
    core_mate = (g // 2) * 2 + (g + 1) % 2
    chip_mate = (g + 2) % groups

    def piece(p):
        return pl.ds(p * part_k, part_k)

    def k_copy(p, m, source, lane, target):
        return remote(
            source, mine.at[m, piece(p)], k_s.at[p, lane, m], k_r.at[p, m], to(c, target)
        )

    def hand_on(p, block):
        @pl.when(jnp.logical_and(is_owner, block // groups == c % per_group))
        def _():
            m = block % groups
            k_copy(p, m, gathered.at[block, piece(p)], 1, chip_mate).start()
            k_copy(p, m, gathered.at[block, piece(p)], 0, core_mate).start()
            mine[m, piece(p)] = gathered[block, piece(p)]

    def line(p, h, zz, target, s, r):
        ref = gathered.at[zz * 2 + y, piece(p)]
        return remote(ref, ref, s.at[p, h], r.at[p, h], to(target, g))

    above_z, below_z = (c + 2) % n, (c + n - 2) % n
    other = z * 2 + (1 - y)

    def y_copy(p, zz, yy):
        ref = gathered.at[zz * 2 + yy, piece(p)]
        return remote(ref, ref, y_s.at[p, zz], y_r.at[p, zz], to(other, g))

    def send_on(p, h, zz, is_up, is_down):
        if is_up:
            @pl.when(z < depth - 1)
            def _():
                line(p, h, zz, above_z, up_s, up_r).start()
        if is_down:
            @pl.when(z > 0)
            def _():
                line(p, h, zz, below_z, down_s, down_r).start()
        y_copy(p, zz, y).start()
        hand_on(p, zz * 2 + y)

    def take_y(p, zz):
        y_copy(p, zz, 1 - y).wait_recv()
        hand_on(p, zz * 2 + (1 - y))

    def stage(p, h):
        if h < depth - 1:
            @pl.when(z - 1 - h >= 0)
            def _():
                line(p, h, z - 1 - h, above_z, up_s, up_r).wait_recv()
                send_on(p, h + 1, z - 1 - h, True, False)

            @pl.when(z + 1 + h <= depth - 1)
            def _():
                line(p, h, z + 1 + h, below_z, down_s, down_r).wait_recv()
                send_on(p, h + 1, z + 1 + h, False, True)
        if h == 0:
            take_y(p, z)
        else:
            @pl.when(z - h >= 0)
            def _():
                take_y(p, z - h)

            @pl.when(z + h <= depth - 1)
            def _():
                take_y(p, z + h)

    early = 1
    for p in range(CHUNKS):
        take_pulses(p)
        transport()
        if p == 0:
            take_averaging()
        jacobian(p)
        send_on(p, 0, z, True, True)
        if p > 0:
            for h in range(early, depth):
                stage(p - 1, h)
        for h in range(early if p < CHUNKS - 1 else depth):
            stage(p, h)

    @pl.when(jnp.logical_not(is_owner))
    def _():
        for p in range(CHUNKS):
            for m in range(groups):
                k_copy(p, m, mine.at[m, piece(p)], 0, core_mate).wait_recv()

                @pl.when(is_relay)
                def _():
                    k_copy(p, m, mine.at[m, piece(p)], 0, core_mate).start()

    left = mine[...].reshape(groups * k, n * obs)
    for b in range(n // 2):
        right = gathered[2 * b : 2 * b + 2].reshape(2 * k, n * obs)
        out_ref[:, 2 * b * k : (2 * b + 2) * k] = lax.dot_general(
            left, right, (((1,), (1,)), ((), ())), preferred_element_type=jnp.float32
        )

    for d in range(1, n):
        a_copy(d, c, (c + d) % n).wait_send()
        m_copy(d, c, (c + d) % n).wait_send()
        for p in range(CHUNKS):
            q_copy(p, d, c, (c + d) % n).wait_send()
        for e in range(1, groups):
            f_copy(d, e, (c + n - d) % n, g, (g + e) % groups).wait_send()
    for p in range(CHUNKS):
        for h in range(depth):
            y_copy(p, h, y).wait_send()
            if h < depth - 1:
                @pl.when(jnp.logical_and(z < depth - 1, z - h >= 0))
                def _():
                    line(p, h, z - h, above_z, up_s, up_r).wait_send()

                @pl.when(jnp.logical_and(z > 0, z + h <= depth - 1))
                def _():
                    line(p, h, z + h, below_z, down_s, down_r).wait_send()
        for m in range(groups):
            @pl.when(is_owner)
            def _():
                k_copy(p, m, mine.at[m, piece(p)], 1, chip_mate).wait_send()

            @pl.when(jnp.logical_or(is_owner, is_relay))
            def _():
                k_copy(p, m, mine.at[m, piece(p)], 0, core_mate).wait_send()


def by_kernel(pulses, wind_x, wind_y, obs_tile, obs_weight, obs_precision):
    n, groups = lax.axis_size("cells"), lax.axis_size("tracers")
    tracers, rows, cols = pulses.shape
    obs, tile_cells = obs_weight.shape
    k = tracers // n
    part_k = k // CHUNKS
    small = jnp.concatenate(
        [
            wind_x,
            wind_y,
            obs_tile.reshape(1, obs).astype(jnp.float32),
            obs_precision.reshape(1, obs).astype(jnp.float32),
            jnp.zeros((2 * 8 - 2 * rows - 2, cols), jnp.float32),
        ],
        axis=0,
    )
    depth = n // 2
    dma = pltpu.SemaphoreType.DMA
    vmem = pl.BlockSpec(memory_space=pltpu.VMEM)
    return pl.pallas_call(
        functools.partial(kernel, n, groups, rows),
        out_shape=jax.ShapeDtypeStruct((groups * k, tracers), jnp.float32),
        in_specs=[vmem] * 3,
        out_specs=vmem,
        scratch_shapes=[
            pltpu.VMEM((CHUNKS, n, rows, part_k, cols), jnp.int16),
            pltpu.VMEM((CHUNKS, n, rows, part_k, cols), jnp.int16),
            pltpu.VMEM((n * rows, part_k, cols), jnp.float32),
            pltpu.VMEM((n * rows, part_k, cols), jnp.float32),
            pltpu.VMEM((n * part_k, rows * cols), jnp.bfloat16),
            pltpu.VMEM((5, n * rows, cols), jnp.float32),
            pltpu.VMEM((n, tile_cells, obs), jnp.bfloat16),
            pltpu.VMEM((n, small.shape[0], obs), jnp.float32),
            pltpu.VMEM((n, k, n * obs), jnp.bfloat16),
            pltpu.VMEM((groups, k, n * obs), jnp.bfloat16),
            dma((CHUNKS, n)), dma((CHUNKS, n)), dma((n,)), dma((n,)), dma((n,)), dma((n,)),
            dma((groups, n)), dma((groups, n)),
            *[dma((CHUNKS, depth))] * 6,
            dma((CHUNKS, 2, groups)), dma((CHUNKS, groups)),
        ],
        compiler_params=pltpu.CompilerParams(
            collective_id=0, has_side_effects=True, vmem_limit_bytes=48 << 20
        ),
        cost_estimate=pl.CostEstimate(
            flops=4 * n * obs * k * groups * tracers, bytes_accessed=8 << 20, transcendentals=0
        ),
    )(pulses.reshape(tracers * rows, cols), small, obs_weight)


def on_device(*args):
    n, groups = lax.axis_size("cells"), lax.axis_size("tracers")
    tracers, rows, cols = args[0].shape
    obs = args[4].shape[0]
    gathered = tracers * n * obs * 2
    fits = gathered <= 4 << 20 and tracers % (n * 16 * CHUNKS) == 0 and rows * 2 + 3 <= 16
    if fits and groups == 4 and n % groups == 0 and rows == 4 and obs == cols == 128:
        return by_kernel(*args)
    return by_collectives(*args)


def solution(mesh):
    placed = (
        P("tracers", "cells", None),
        P("cells", None),
        P("cells", None),
        P("cells", None),
        P("cells", None),
        P("cells"),
    )
    return jax.shard_map(
        on_device, mesh=mesh, in_specs=placed, out_specs=P("cells", "tracers"), check_vma=False
    )
```
